128 devices in a mesh: row: 16 (over z_hi, y, core), field: 8 (over z_lo, x).
Axes of the slice: x: 4, y: 4, z: 4 (z_hi: 2, z_lo: 2; z = z_hi * 2 + z_lo), core: 2. Of those that a mesh axis runs over, the one named last changes fastest.
Arguments:
- rhs: bfloat16 [8, 16, 512, 4096], P(None, 'row', None, 'field'), may hold values from -6 to 6
- factor: bfloat16 [8, 16, 512, 1536], P(None, 'row'), may hold values from -0.25 to 0.25
- pivot_map: int32 [1536], replicated, may hold values from 0 to 2, as said below
- pivot_diag: float32 [1536], P('field'), may hold values from -2 to 2, as said below
- pivot_off: float32 [1536], P('field'), may hold values from -4 to 4, as said below
- perm: int32 [3, 512], replicated, may hold values from 0 to 511, each once within a row
Outputs:
- result: float32 [8, 16, 512, 4096], P(None, 'row', None, 'field')
The draws below stay inside these ranges and needn't reach their ends.
Inputs may be any that keep to these rules, and one draw needn't show every extreme that they name: `pivot_map`: every 1 is followed by a 2 and every 2 follows a 1; no 2x2 block crosses the end of a panel. `pivot_diag`: magnitudes from 1 to 2, either sign. `pivot_off`: magnitudes from 2.5 to 4, either sign.
All inputs are finite; a program needn't handle non-finite values.
Results may differ from the reference program's by a relative error of at most 0.0038.
Values may be sent and summed in bfloat16 or wider, within the bound.
A program may use at most 128 MiB of HBM per device.

```python
import jax
import jax.numpy as jnp
from jax import lax

NB = 512
BLK_DEV = 8
PANELS = 3
COLS = 4096
N_ROW = 16


def draw_pivot_map(key, part):
    key = jax.random.fold_in(key, 11)
    coin_flips = jax.random.randint(key, (PANELS, NB), 0, 2).astype(jnp.int32)
    final_row = (jnp.arange(NB) == NB - 1).astype(jnp.int32)

    def advance(previous, pair_item):
        coin, ending = pair_item
        code = jnp.where(previous == 1, 2, jnp.where((coin == 1) & (ending == 0), 1, 0)).astype(jnp.int32)
        return (code, code)

    def per_panel(flips):
        _, codes_out = lax.scan(advance, jnp.int32(0), (flips, final_row))
        return codes_out
    return jax.vmap(per_panel)(coin_flips).reshape(PANELS * NB).astype(jnp.int32)


def signed_magnitudes(key, low, spread):
    key_sign, key_size = jax.random.split(key)
    uniform_draw = jax.random.uniform(key_size, (PANELS * NB,), jnp.float32)
    sign_draw = jnp.where(jax.random.randint(key_sign, (PANELS * NB,), 0, 2) == 1, 1.0, -1.0)
    return (sign_draw, uniform_draw, low, spread)


def draw_pivot_diag(key, part):
    key = jax.random.fold_in(key, 23)
    sign_draw, uniform_draw, low, spread = signed_magnitudes(key, 1.0, 1.0)
    magnitude = low + uniform_draw
    return (sign_draw * magnitude).astype(jnp.float32)


def draw_pivot_off(key, part):
    key = jax.random.fold_in(key, 37)
    sign_draw, uniform_draw, low, spread = signed_magnitudes(key, 2.5, 1.5)
    magnitude = low + spread * uniform_draw
    return (sign_draw * magnitude).astype(jnp.float32)


def block_scale(stream_key, shape, pieces, low, largest):
    level = 1.0
    for axis_at, shards_of in pieces:
        draws = jax.random.uniform(jax.random.fold_in(jax.random.fold_in(stream_key, 6), axis_at), (shards_of,), jnp.float32, low / len(pieces), largest / len(pieces))
        level = level * jnp.repeat(jnp.exp(draws), shape[axis_at] // shards_of).reshape((-1,) + (1,) * (len(shape) - 1 - axis_at))
    return level


def bell_draw(own_key, shape, scale, reach, shards=(), kind=jnp.bfloat16):
    entries = scale * jax.random.normal(own_key, shape, jnp.float32)
    if shards:
        entries = entries * block_scale(own_key, shape, shards, -0.22, 0.18)
    return jnp.clip(entries, -reach, reach).astype(kind)


def setup_inputs(seed: int = 0) -> dict:
    streams_of = jax.random.split(jax.random.key(seed), 7)
    return {
        "rhs": bell_draw(streams_of[0], (BLK_DEV, N_ROW, NB, COLS), 1.0, 6.0, ((1, 16), (3, 8))),
        "factor": bell_draw(streams_of[1], (BLK_DEV, N_ROW, NB, PANELS * NB), NB ** -0.5, 0.25, ((1, 16),)),
        "pivot_map": draw_pivot_map(jax.random.fold_in(streams_of[6], 71), 0),
        "pivot_diag": draw_pivot_diag(jax.random.fold_in(streams_of[6], 71), 0),
        "pivot_off": draw_pivot_off(jax.random.fold_in(streams_of[6], 71), 0),
        "perm": jax.vmap(lambda own: jax.random.permutation(own, NB))(jax.random.split(streams_of[5], PANELS)).reshape((PANELS, NB)).astype(jnp.int32),
    }


def solve_block(diagonal_block, panel_rows):
    return jax.scipy.linalg.solve_triangular(diagonal_block.astype(jnp.float32), panel_rows, lower=True, unit_diagonal=True)

def scale_pivots(solved, pivot_codes, diagonal, coupling):
    later_rows = jnp.roll(solved, -1, 0)
    earlier_rows = jnp.roll(solved, 1, 0)
    diagonal_next = jnp.roll(diagonal, -1)
    diagonal_prior = jnp.roll(diagonal, 1)
    coupling_prior = jnp.roll(coupling, 1)
    opens_pair = pivot_codes == 1
    closes_pair = pivot_codes == 2
    self_coef = jnp.where(opens_pair, diagonal_next, jnp.where(closes_pair, diagonal_prior, 1.0))
    next_coef = jnp.where(opens_pair, -coupling, 0.0)
    prior_coef = jnp.where(closes_pair, -coupling_prior, 0.0)
    denominator = jnp.where(opens_pair, diagonal * diagonal_next - coupling * coupling, jnp.where(closes_pair, diagonal_prior * diagonal - coupling_prior * coupling_prior, diagonal))
    total_rows = self_coef[:, None] * solved + next_coef[:, None] * later_rows + prior_coef[:, None] * earlier_rows
    return total_rows / denominator[:, None]

def reference(rhs, factor, pivot_map, pivot_diag, pivot_off, perm):
    total = BLK_DEV * N_ROW
    residual_rows = rhs.astype(jnp.float32).reshape(total, NB, COLS)
    factor_rows = factor.reshape(total, NB, PANELS * NB)
    for panel_index in range(PANELS):
        residual_rows = residual_rows.at[panel_index].set(residual_rows[panel_index][perm[panel_index]])
    global_block = jnp.arange(total, dtype=jnp.int32)
    for panel_index in range(PANELS):
        start = panel_index * NB
        columns = factor_rows[:, :, start:start + NB]
        solved = solve_block(columns[panel_index], residual_rows[panel_index])
        scaled = scale_pivots(solved, pivot_map[start:start + NB], pivot_diag[start:start + NB], pivot_off[start:start + NB])
        solved_low = lax.optimization_barrier(solved.astype(jnp.bfloat16)).astype(jnp.float32)
        update = jnp.dot(columns.reshape(total * NB, NB).astype(jnp.float32), solved_low, precision=lax.Precision.HIGHEST).reshape(total, NB, COLS)
        residual_rows = residual_rows - jnp.where((global_block > panel_index)[:, None, None], update, 0.0)
        residual_rows = residual_rows.at[panel_index].set(scaled)
    return residual_rows.reshape(BLK_DEV, N_ROW, NB, COLS)
```

```python
import jax
import jax.numpy as jnp
from jax import lax
from jax.experimental import pallas as pl
from jax.experimental.pallas import tpu as pltpu
from jax.sharding import PartitionSpec as P

MESH = pl.DeviceIdType.MESH
F32, BF16 = jnp.float32, jnp.bfloat16
NB, PANELS, BLOCKS = 512, 3, 8
HALF = 256
CHUNK = 128
CHUNKS = 4
FIELDS, ROWS = 8, 16
DPART = 192


def dot(a, b):
    return jnp.dot(a, b, preferred_element_type=F32)


def split(a):
    high = a.astype(BF16)
    return high, (a - high.astype(F32)).astype(BF16)


def dot2(a, b):
    return dot(a[0], b) + dot(a[1], b)


def dot2r(a, b):
    return dot(a, b[0]) + dot(a, b[1])


def dot3(a, b):
    return dot(a[0], b[0]) + (dot(a[0], b[1]) + dot(a[1], b[0]))


def invert_tiles(tiles):
    rows = lax.broadcasted_iota(jnp.int32, (256, 256), 0)
    cols = lax.broadcasted_iota(jnp.int32, (256, 256), 1)
    eye = jnp.where(rows == cols, 1.0, 0.0)
    base = (rows > cols) & (rows // 16 == cols // 16)
    n1 = [jnp.where(base, t, 0.0) for t in tiles]
    n1b = [n.astype(BF16) for n in n1]
    n2 = [dot(n, n) for n in n1b]
    n2s = [split(n) for n in n2]
    n4 = [dot3(s, s) for s in n2s]
    x = [eye - a + b - dot2r(ab, bs) for a, b, ab, bs in zip(n1, n2, n1b, n2s)]
    n4s = [split(n) for n in n4]
    n8s = [split(dot3(s, s)) for s in n4s]
    x = [a + dot3(split(a), s) for a, s in zip(x, n4s)]
    x = [a + dot3(split(a), s) for a, s in zip(x, n8s)]
    size = 16
    while size < 256:
        off = (rows // (2 * size) == cols // (2 * size)) & (rows // size > cols // size)
        es = [jnp.where(off, t, 0.0).astype(BF16) for t in tiles]
        xs = [split(a) for a in x]
        ys = [split(dot2r(e, s)) for e, s in zip(es, xs)]
        x = [a - dot3(s, y) for a, s, y in zip(x, xs, ys)]
        size *= 2
    return x


def kernel(rhs, factor, pmap, pdiag, poff, perm, out, fac, b, w, xh, xl, c, m0h, m0l, m1h, m1l,
           coef, dsend, dall, load_sem, send_sem, recv_sem, core_sem, dsend_sem, drecv_sem):
    r = lax.axis_index("row")
    f = lax.axis_index("field")
    solver = r < PANELS
    mate = r + 1 - 2 * lax.rem(r, 2)

    barrier = pltpu.get_barrier_semaphore()
    for k in range(1, ROWS):
        pl.semaphore_signal(barrier, inc=1, device_id=(lax.rem(r + k, ROWS), f), device_id_type=MESH)

    @pl.when(solver)
    def _():
        for k in range(1, FIELDS):
            pl.semaphore_signal(barrier, inc=1, device_id=(r, lax.rem(f + k, FIELDS)), device_id_type=MESH)

    loads = []
    for l in range(BLOCKS):
        loads.append(pltpu.make_async_copy(factor.at[l, 0], fac.at[l], load_sem.at[0, l]))
        loads.append(pltpu.make_async_copy(rhs.at[l, 0], b.at[l], load_sem.at[1, l]))
        loads[-2].start()
        loads[-1].start()

    def wslot(p, j):
        return w.at[p, j // 2, :, pl.ds((j % 2) * CHUNK, CHUNK)]

    def send(p, j, k, dst):
        return pltpu.make_async_remote_copy(
            wslot(p, j), wslot(p, j), send_sem.at[p, j, k], recv_sem.at[p, j],
            device_id=(dst, f), device_id_type=MESH)

    def to_mate(p, j):
        return pltpu.make_async_remote_copy(
            wslot(p, j), wslot(p, j), core_sem.at[p, j], recv_sem.at[p, j],
            device_id=(mate, f), device_id_type=MESH)

    ICI = [
        [(0, (2, 6, 8)), (2, (4,)), (8, (10, 14)), (10, (12,))],
        [(1, (2, 6, 8)), (2, (4,)), (8, (10, 14)), (10, (12,))],
        [(2, (10, 0, 6, 4)), (10, (14, 8, 12))],
    ]

    def core_sender(p):
        even = lax.rem(r, 2) == 0
        if p == 1:
            return (r == 1) | (even & (r > 0))
        return even

    def forward(p, j):
        for src, dsts in ICI[p]:
            @pl.when(r == src)
            def _():
                for k, dst in enumerate(dsts):
                    send(p, j, k, dst).start()

        @pl.when(core_sender(p))
        def _():
            to_mate(p, j).start()

    def arrive(p, j):
        @pl.when(r != p)
        def _():
            to_mate(p, j).wait_recv()

    loads[0].wait()
    loads[1].wait()

    @pl.when(solver)
    def _():
        own = pl.multiple_of(r * NB, NB)
        tiles = [fac[0, t * 256:(t + 1) * 256, pl.ds(own + t * 256, 256)].astype(F32) for t in range(2)]
        x11, x22 = invert_tiles(tiles)
        l21 = fac[0, 256:512, pl.ds(own, 256)]
        x11s, x22s = split(x11), split(x22)
        x21s = split(-dot3(x22s, split(dot2r(l21, x11s))))
        zero = jnp.zeros((256, 256), BF16)
        for ref, k in ((xh, 0), (xl, 1)):
            ref[0:256, 0:256] = x11s[k]
            ref[0:256, 256:512] = zero
            ref[256:512, 0:256] = x21s[k]
            ref[256:512, 256:512] = x22s[k]

        def apply_x(right):
            top = dot(xh[0:256, 0:256], right[0:256]) + dot(xl[0:256, 0:256], right[0:256])
            low = dot(xh[256:512, :], right) + dot(xl[256:512, :], right)
            return top, low

        dsend[...] = jnp.zeros_like(dsend)
        dsend[0:1, 0:DPART] = pdiag[...].reshape(1, DPART)
        dsend[1:2, 0:DPART] = poff[...].reshape(1, DPART)

        which = lax.broadcasted_iota(jnp.int32, (128, NB), 0)
        prow = jnp.where(r == 0, perm[0:1, :], jnp.where(r == 1, perm[1:2, :], perm[2:3, :]))
        pcol = jnp.where(which == 0, prow.astype(F32), 0.0).T[:, 0:1].astype(jnp.int32)
        onehot = jnp.where(lax.broadcasted_iota(jnp.int32, (NB, NB), 1) == pcol, 1.0, 0.0).astype(BF16)
        pb = dot(onehot, b[0]).astype(BF16)
        top, low = apply_x(pb)
        c[0:256, :] = top
        c[256:512, :] = low

        @pl.when(r >= 1)
        def _():
            for k, part in enumerate(apply_x(fac[0, :, 0:NB])):
                m0h[k * 256:(k + 1) * 256, :], m0l[k * 256:(k + 1) * 256, :] = split(part)

        @pl.when(r >= 2)
        def _():
            for k, part in enumerate(apply_x(fac[0, :, NB:2 * NB])):
                m1h[k * 256:(k + 1) * 256, :], m1l[k * 256:(k + 1) * 256, :] = split(part)

    @pl.when(solver)
    def _():
        pl.semaphore_wait(barrier, ROWS - 1 + FIELDS - 1)

    @pl.when(jnp.logical_not(solver))
    def _():
        pl.semaphore_wait(barrier, ROWS - 1)

    def cols(j):
        return slice(j * CHUNK, (j + 1) * CHUNK)

    def wcols(p, j):
        return w[p, j // 2, :, (j % 2) * CHUNK:(j % 2 + 1) * CHUNK]

    def emit(p, j, z):
        out[0, 0, :, cols(j)] = z
        w[p, j // 2, :, (j % 2) * CHUNK:(j % 2 + 1) * CHUNK] = z.astype(BF16)

    def trailing01(h):
        first = jnp.where(solver, 1, 0)
        sl = slice(h * HALF, (h + 1) * HALF)

        def step(l, carry):
            out[l, 0, :, sl] = b[l, :, sl].astype(F32) - (
                dot(fac[l, :, 0:NB], w[0, h]) + dot(fac[l, :, NB:2 * NB], w[1, h]))
            return carry
        lax.fori_loop(first, BLOCKS, step, 0)

    def trailing2(h):
        first = jnp.where(solver, 1, 0)
        sl = slice(h * HALF, (h + 1) * HALF)

        def step(l, carry):
            out[l, 0, :, sl] = out[l, 0, :, sl] - dot(fac[l, :, 2 * NB:3 * NB], w[2, h])
            return carry
        lax.fori_loop(first, BLOCKS, step, 0)

    def rest_loaded():
        for copy in loads[2:]:
            copy.wait()

    for j in range(CHUNKS):
        @pl.when(r == 0)
        def _():
            emit(0, j, c[:, cols(j)])
        arrive(0, j)
        forward(0, j)

        @pl.when(r == 1)
        def _():
            wj = wcols(0, j)
            emit(1, j, c[:, cols(j)] - (dot(m0h[...], wj) + dot(m0l[...], wj)))

        @pl.when(r != 0)
        def _():
            arrive(1, j)
            forward(1, j)

        @pl.when(r == 2)
        def _():
            w0, w1 = wcols(0, j), wcols(1, j)
            emit(2, j, c[:, cols(j)] - ((dot(m0h[...], w0) + dot(m0l[...], w0))
                                       + (dot(m1h[...], w1) + dot(m1l[...], w1))))
            forward(2, j)

    @pl.when(r == 0)
    def _():
        for j in range(CHUNKS):
            arrive(1, j)

    def dcopy(k):
        return pltpu.make_async_remote_copy(
            dsend, dall.at[f], dsend_sem.at[k], drecv_sem.at[f],
            device_id=(r, lax.rem(f + k, FIELDS)), device_id_type=MESH)

    def darrival(k):
        src = lax.rem(f + k, FIELDS)
        return pltpu.make_async_remote_copy(
            dsend, dall.at[src], dsend_sem.at[k], drecv_sem.at[src],
            device_id=(r, src), device_id_type=MESH)

    @pl.when(solver)
    def _():
        for k in range(1, FIELDS):
            dcopy(k).start()

    rest_loaded()
    trailing01(0)
    trailing01(1)

    for j in range(CHUNKS):
        @pl.when(r != 2)
        def _():
            arrive(2, j)
            forward(2, j)
        if j == 1:
            trailing2(0)

    trailing2(1)

    @pl.when(solver)
    def _():
        for k in range(1, FIELDS):
            darrival(k).wait_recv()
        for k in range(1, FIELDS):
            dcopy(k).wait_send()
        wide = jnp.zeros((8, PANELS * NB), F32)
        pad = jnp.zeros((8, PANELS * NB - 256), F32)
        for k in range(FIELDS):
            part = jnp.where(f == k, dsend[...], dall[k])
            row = jnp.concatenate([part, pad], axis=1)
            wide = wide + (pltpu.roll(row, k * DPART, 1) if k else row)

        def mine(a):
            return jnp.where(r == 0, a[:, 0:NB], jnp.where(r == 1, a[:, NB:2 * NB], a[:, 2 * NB:3 * NB]))
        both = mine(wide)
        diag, off = both[0:1], both[1:2]
        code = mine(pmap[...].reshape(1, PANELS * NB))
        diag8 = jnp.broadcast_to(diag, (8, NB))
        off8 = jnp.broadcast_to(off, (8, NB))
        code8 = jnp.broadcast_to(code, (8, NB))
        after, before = pltpu.roll(diag8, NB - 1, 1), pltpu.roll(diag8, 1, 1)
        off_before = pltpu.roll(off8, 1, 1)
        opens, closes = code8 == 1, code8 == 2
        den = jnp.where(opens, diag8 * after - off8 * off8,
                        jnp.where(closes, before * diag8 - off_before * off_before, diag8))
        own_c = jnp.where(opens, after, jnp.where(closes, before, 1.0)) / den
        next_c = jnp.where(opens, -off8, 0.0) / den
        prior_c = jnp.where(closes, -off_before, 0.0) / den
        which = lax.broadcasted_iota(jnp.int32, (128, NB), 0)
        stack = jnp.where(which == 0, own_c[0:1], jnp.where(which == 1, next_c[0:1],
                          jnp.where(which == 2, prior_c[0:1], 0.0)))
        coef[...] = stack.T
        own_k, next_k, prior_k = coef[:, 0:1], coef[:, 1:2], coef[:, 2:3]
        for j in range(CHUNKS):
            z = out[0, 0, :, cols(j)]
            out[0, 0, :, cols(j)] = (own_k * z + next_k * pltpu.roll(z, NB - 1, 0)
                                     + prior_k * pltpu.roll(z, 1, 0))

    for p in range(PANELS):
        for j in range(CHUNKS):
            for src, dsts in ICI[p]:
                @pl.when(r == src)
                def _():
                    for k, dst in enumerate(dsts):
                        send(p, j, k, dst).wait_send()

            @pl.when(core_sender(p))
            def _():
                to_mate(p, j).wait_send()


def local(rhs, factor, pivot_map, pivot_diag, pivot_off, perm):
    vmem = pl.BlockSpec(memory_space=pltpu.VMEM)
    hbm = pl.BlockSpec(memory_space=pltpu.HBM)
    return pl.pallas_call(
        kernel,
        out_shape=jax.ShapeDtypeStruct((BLOCKS, 1, NB, NB), F32),
        in_specs=[hbm, hbm, vmem, vmem, vmem, vmem],
        out_specs=vmem,
        scratch_shapes=[
            pltpu.VMEM((BLOCKS, NB, PANELS * NB), BF16),
            pltpu.VMEM((BLOCKS, NB, NB), BF16),
            pltpu.VMEM((PANELS, 2, NB, HALF), BF16),
            pltpu.VMEM((NB, NB), BF16), pltpu.VMEM((NB, NB), BF16),
            pltpu.VMEM((NB, NB), F32),
            pltpu.VMEM((NB, NB), BF16), pltpu.VMEM((NB, NB), BF16),
            pltpu.VMEM((NB, NB), BF16), pltpu.VMEM((NB, NB), BF16),
            pltpu.VMEM((NB, 128), F32),
            pltpu.VMEM((8, 256), F32), pltpu.VMEM((FIELDS, 8, 256), F32),
            pltpu.SemaphoreType.DMA((2, BLOCKS)),
            pltpu.SemaphoreType.DMA((PANELS, CHUNKS, 4)),
            pltpu.SemaphoreType.DMA((PANELS, CHUNKS)),
            pltpu.SemaphoreType.DMA((PANELS, CHUNKS)),
            pltpu.SemaphoreType.DMA((FIELDS,)), pltpu.SemaphoreType.DMA((FIELDS,)),
        ],
        compiler_params=pltpu.CompilerParams(
            collective_id=0, has_side_effects=True, vmem_limit_bytes=38 << 20),
        cost_estimate=pl.CostEstimate(flops=2 * 4096 * 1536 * 512, bytes_accessed=24 << 20, transcendentals=0),
    )(rhs, factor, pivot_map, pivot_diag, pivot_off, perm)


def solution(mesh):
    placed = (
        P(None, "row", None, "field"),
        P(None, "row", None, None),
        P(),
        P("field"),
        P("field"),
        P(),
    )
    return jax.shard_map(
        local, mesh=mesh, in_specs=placed, out_specs=P(None, "row", None, "field"), check_vma=False
    )
```

```python
import jax
import jax.numpy as jnp
from jax import lax
from jax.experimental import pallas as pl
from jax.experimental.pallas import tpu as pltpu
from jax.sharding import PartitionSpec as P

MESH = pl.DeviceIdType.MESH
F32, BF16 = jnp.float32, jnp.bfloat16
NB, PANELS, BLOCKS = 512, 3, 8
HALF = 256
CHUNK = 128
CHUNKS = 4
FIELDS, ROWS = 8, 16
DPART = 192


def dot(a, b):
    return jnp.dot(a, b, preferred_element_type=F32)


def split(a):
    high = a.astype(BF16)
    return high, (a - high.astype(F32)).astype(BF16)


def dot2(a, b):
    return dot(a[0], b) + dot(a[1], b)


def dot2r(a, b):
    return dot(a, b[0]) + dot(a, b[1])


def dot3(a, b):
    return dot(a[0], b[0]) + (dot(a[0], b[1]) + dot(a[1], b[0]))


def invert_tiles(tiles):
    rows = lax.broadcasted_iota(jnp.int32, (256, 256), 0)
    cols = lax.broadcasted_iota(jnp.int32, (256, 256), 1)
    eye = jnp.where(rows == cols, 1.0, 0.0)
    base = (rows > cols) & (rows // 16 == cols // 16)
    n1 = [jnp.where(base, t, 0.0) for t in tiles]
    n1b = [n.astype(BF16) for n in n1]
    n2 = [dot(n, n) for n in n1b]
    n2s = [split(n) for n in n2]
    n4 = [dot3(s, s) for s in n2s]
    x = [eye - a + b - dot2r(ab, bs) for a, b, ab, bs in zip(n1, n2, n1b, n2s)]
    n4s = [split(n) for n in n4]
    n8s = [split(dot3(s, s)) for s in n4s]
    x = [a + dot3(split(a), s) for a, s in zip(x, n4s)]
    x = [a + dot3(split(a), s) for a, s in zip(x, n8s)]
    size = 16
    while size < 256:
        off = (rows // (2 * size) == cols // (2 * size)) & (rows // size > cols // size)
        es = [jnp.where(off, t, 0.0).astype(BF16) for t in tiles]
        xs = [split(a) for a in x]
        ys = [split(dot2r(e, s)) for e, s in zip(es, xs)]
        x = [a - dot3(s, y) for a, s, y in zip(x, xs, ys)]
        size *= 2
    return x


def kernel(rhs, factor, pmap_hbm, pdiag_hbm, poff_hbm, perm_hbm, out, fac, b, w, xh, xl, c,
           m0h, m0l, m1h, m1l, coef, dsend, dall, pmap, pdiag, poff, perm,
           load_sem, small_sem, send_sem, recv_sem, core_sem, dsend_sem, drecv_sem):
    r = lax.axis_index("row")
    f = lax.axis_index("field")
    even = lax.rem(r, 2) == 0
    odd = jnp.logical_not(even)
    solver = r < PANELS
    mate = r + 1 - 2 * lax.rem(r, 2)

    loads = []
    for l in range(BLOCKS):
        loads.append(pltpu.make_async_copy(factor.at[l, 0], fac.at[l], load_sem.at[0, l]))
        loads.append(pltpu.make_async_copy(rhs.at[l, 0], b.at[l], load_sem.at[1, l]))
    small = [pltpu.make_async_copy(src, dst, small_sem.at[k]) for k, (src, dst) in enumerate(
        ((perm_hbm, perm), (pmap_hbm, pmap), (pdiag_hbm, pdiag), (poff_hbm, poff)))]
    loads[0].start()
    for copy in small:
        copy.start()
    loads[1].start()

    barrier = pltpu.get_barrier_semaphore()
    for k in range(1, ROWS):
        pl.semaphore_signal(barrier, inc=1, device_id=(lax.rem(r + k, ROWS), f), device_id_type=MESH)

    @pl.when(solver)
    def _():
        for k in range(1, FIELDS):
            pl.semaphore_signal(barrier, inc=1, device_id=(r, lax.rem(f + k, FIELDS)), device_id_type=MESH)

    def wslot(p, j):
        return w.at[p, j // 2, :, pl.ds((j % 2) * CHUNK, CHUNK)]

    def send(p, j, k, dst):
        return pltpu.make_async_remote_copy(
            wslot(p, j), wslot(p, j), send_sem.at[p, j, k], recv_sem.at[p, j],
            device_id=(dst, f), device_id_type=MESH)

    def to_mate(p, j):
        return pltpu.make_async_remote_copy(
            wslot(p, j), wslot(p, j), core_sem.at[p, j], recv_sem.at[p, j],
            device_id=(mate, f), device_id_type=MESH)

    EARLY = ((6, (4, 14)), (4, (12,)), (8, (10,)))
    ICI = [((0, (2, 6, 8)),) + EARLY, ((1, (2, 6, 8)),) + EARLY,
           ((2, (11, 1, 5)), (1, (7, 9)), (11, (15, 13)))]

    def core_sender(p):
        if p == 0:
            return even
        if p == 1:
            return (r == 1) | (even & (r > 0))
        return (r == 2) | (odd & (r != 3))

    def forward(p, j, *rows):
        for src, dsts in ICI[p]:
            if src in rows:
                @pl.when(r == src)
                def _():
                    for k, dst in enumerate(dsts):
                        send(p, j, k, dst).start()

    def arrive(p, j):
        to_mate(p, j).wait_recv()

    for copy in small + loads[:2]:
        copy.wait()
    for copy in loads[2:]:
        copy.start()

    @pl.when(solver)
    def _():
        which = lax.broadcasted_iota(jnp.int32, (128, NB), 0)
        prow = jnp.where(r == 0, perm[0:1, :], jnp.where(r == 1, perm[1:2, :], perm[2:3, :]))
        pcol = jnp.where(which == 0, prow.astype(F32), 0.0).T[:, 0:1].astype(jnp.int32)
        onehot = jnp.where(lax.broadcasted_iota(jnp.int32, (NB, NB), 1) == pcol, 1.0, 0.0).astype(BF16)
        pb = dot(onehot, b[0]).astype(BF16)

        own = pl.multiple_of(r * NB, NB)
        tiles = [fac[0, t * 256:(t + 1) * 256, pl.ds(own + t * 256, 256)].astype(F32) for t in range(2)]
        x11, x22 = invert_tiles(tiles)
        l21 = fac[0, 256:512, pl.ds(own, 256)]
        x11s, x22s = split(x11), split(x22)
        x21s = split(-dot3(x22s, split(dot2r(l21, x11s))))
        zero = jnp.zeros((256, 256), BF16)
        for ref, k in ((xh, 0), (xl, 1)):
            ref[0:256, 0:256] = x11s[k]
            ref[0:256, 256:512] = zero
            ref[256:512, 0:256] = x21s[k]
            ref[256:512, 256:512] = x22s[k]

        def apply_x(right):
            top = dot(xh[0:256, 0:256], right[0:256]) + dot(xl[0:256, 0:256], right[0:256])
            low = dot(xh[256:512, :], right) + dot(xl[256:512, :], right)
            return top, low

        top, low = apply_x(pb)
        c[0:256, :] = top
        c[256:512, :] = low

        @pl.when(r >= 1)
        def _():
            for k, part in enumerate(apply_x(fac[0, :, 0:NB])):
                m0h[k * 256:(k + 1) * 256, :], m0l[k * 256:(k + 1) * 256, :] = split(part)

        @pl.when(r >= 2)
        def _():
            for k, part in enumerate(apply_x(fac[0, :, NB:2 * NB])):
                m1h[k * 256:(k + 1) * 256, :], m1l[k * 256:(k + 1) * 256, :] = split(part)

        pl.semaphore_wait(barrier, ROWS - 1 + FIELDS - 1)

    @pl.when(jnp.logical_not(solver))
    def _():
        pl.semaphore_wait(barrier, ROWS - 1)

    def cols(j):
        return slice(j * CHUNK, (j + 1) * CHUNK)

    def wcols(p, j):
        return w[p, j // 2, :, (j % 2) * CHUNK:(j % 2 + 1) * CHUNK]

    def emit(p, j, z):
        out[0, 0, :, cols(j)] = z
        w[p, j // 2, :, (j % 2) * CHUNK:(j % 2 + 1) * CHUNK] = z.astype(BF16)

    def on_blocks(step):
        pl.when(jnp.logical_not(solver))(lambda: step(0))
        for l in range(1, BLOCKS):
            step(l)

    def trailing01(h):
        sl = slice(h * HALF, (h + 1) * HALF)

        def step(l):
            out[l, 0, :, sl] = b[l, :, sl].astype(F32) - (
                dot(fac[l, :, 0:NB], w[0, h]) + dot(fac[l, :, NB:2 * NB], w[1, h]))
        on_blocks(step)

    def trailing2(h):
        sl = slice(h * HALF, (h + 1) * HALF)

        def step(l):
            out[l, 0, :, sl] = out[l, 0, :, sl] - dot(fac[l, :, 2 * NB:3 * NB], w[2, h])
        on_blocks(step)

    @pl.when(r == 0)
    def _():
        for j in range(CHUNKS):
            emit(0, j, c[:, cols(j)])
            to_mate(0, j).start()
            forward(0, j, 0)

    @pl.when(r == 1)
    def _():
        for j in range(CHUNKS):
            arrive(0, j)
            wj = wcols(0, j)
            emit(1, j, c[:, cols(j)] - (dot(m0h[...], wj) + dot(m0l[...], wj)))
            forward(1, j, 1)
            to_mate(1, j).start()

    @pl.when(r == 2)
    def _():
        for j in range(CHUNKS):
            arrive(0, j)
            to_mate(0, j).start()
            arrive(1, j)
            to_mate(1, j).start()
            w0, w1 = wcols(0, j), wcols(1, j)
            emit(2, j, c[:, cols(j)] - ((dot(m0h[...], w0) + dot(m0l[...], w0))
                                       + (dot(m1h[...], w1) + dot(m1l[...], w1))))
            forward(2, j, 2)
            to_mate(2, j).start()

    @pl.when(even & (r >= 4) & (r <= 8))
    def _():
        for j in range(CHUNKS):
            for p in range(2):
                arrive(p, j)
                forward(p, j, 4, 6, 8)
                to_mate(p, j).start()

    def from_two(js):
        @pl.when(even & (r >= 10))
        def _():
            for j in js:
                for p in range(2):
                    arrive(p, j)
                    to_mate(p, j).start()

        @pl.when(odd & (r >= 3))
        def _():
            for j in js:
                for p in range(2):
                    arrive(p, j)

        @pl.when(r == 0)
        def _():
            for j in js:
                arrive(1, j)

    def passing(js):
        for j in js:
            arrive(2, j)
            forward(2, j, 1, 11)

            @pl.when(r != 3)
            def _():
                to_mate(2, j).start()

    def dcopy(k):
        return pltpu.make_async_remote_copy(
            dsend, dall.at[f], dsend_sem.at[k], drecv_sem.at[f],
            device_id=(r, lax.rem(f + k, FIELDS)), device_id_type=MESH)

    def darrival(k):
        src = lax.rem(f + k, FIELDS)
        return pltpu.make_async_remote_copy(
            dsend, dall.at[src], dsend_sem.at[k], drecv_sem.at[src],
            device_id=(r, src), device_id_type=MESH)

    @pl.when(solver)
    def _():
        dsend[...] = jnp.zeros_like(dsend)
        dsend[0:1, 0:DPART] = pdiag[...].reshape(1, DPART)
        dsend[1:2, 0:DPART] = poff[...].reshape(1, DPART)
        for k in range(1, FIELDS):
            dcopy(k).start()

    for copy in loads[2:]:
        copy.wait()

    @pl.when(r == 11)
    def _():
        passing(range(CHUNKS))

    from_two((0, 1))
    trailing01(0)
    from_two((2, 3))
    trailing01(1)

    @pl.when(solver)
    def _():
        for k in range(1, FIELDS):
            darrival(k).wait_recv()
        for k in range(1, FIELDS):
            dcopy(k).wait_send()
        wide = jnp.zeros((8, PANELS * NB), F32)
        pad = jnp.zeros((8, PANELS * NB - 256), F32)
        for k in range(FIELDS):
            part = jnp.where(f == k, dsend[...], dall[k])
            row = jnp.concatenate([part, pad], axis=1)
            wide = wide + (pltpu.roll(row, k * DPART, 1) if k else row)

        def mine(a):
            return jnp.where(r == 0, a[:, 0:NB], jnp.where(r == 1, a[:, NB:2 * NB], a[:, 2 * NB:3 * NB]))
        both = mine(wide)
        diag, off = both[0:1], both[1:2]
        code = mine(pmap[...].reshape(1, PANELS * NB))
        diag8 = jnp.broadcast_to(diag, (8, NB))
        off8 = jnp.broadcast_to(off, (8, NB))
        code8 = jnp.broadcast_to(code, (8, NB))
        after, before = pltpu.roll(diag8, NB - 1, 1), pltpu.roll(diag8, 1, 1)
        off_before = pltpu.roll(off8, 1, 1)
        opens, closes = code8 == 1, code8 == 2
        den = jnp.where(opens, diag8 * after - off8 * off8,
                        jnp.where(closes, before * diag8 - off_before * off_before, diag8))
        own_c = jnp.where(opens, after, jnp.where(closes, before, 1.0)) / den
        next_c = jnp.where(opens, -off8, 0.0) / den
        prior_c = jnp.where(closes, -off_before, 0.0) / den
        which = lax.broadcasted_iota(jnp.int32, (128, NB), 0)
        stack = jnp.where(which == 0, own_c[0:1], jnp.where(which == 1, next_c[0:1],
                          jnp.where(which == 2, prior_c[0:1], 0.0)))
        coef[...] = stack.T
        own_k, next_k, prior_k = coef[:, 0:1], coef[:, 1:2], coef[:, 2:3]
        for j in range(CHUNKS):
            z = out[0, 0, :, cols(j)]
            out[0, 0, :, cols(j)] = (own_k * z + next_k * pltpu.roll(z, NB - 1, 0)
                                     + prior_k * pltpu.roll(z, 1, 0))

    @pl.when(r == 1)
    def _():
        passing(range(CHUNKS))

    plain = odd & (r != 1) & (r != 11)
    for h in range(2):
        @pl.when(plain)
        def _():
            passing((2 * h, 2 * h + 1))

        @pl.when(even & (r != 2))
        def _():
            for j in (2 * h, 2 * h + 1):
                arrive(2, j)
        trailing2(h)

    for p in range(PANELS):
        for j in range(CHUNKS):
            for src, dsts in ICI[p]:
                @pl.when(r == src)
                def _():
                    for k, dst in enumerate(dsts):
                        send(p, j, k, dst).wait_send()

            @pl.when(core_sender(p))
            def _():
                to_mate(p, j).wait_send()


def local(rhs, factor, pivot_map, pivot_diag, pivot_off, perm):
    vmem = pl.BlockSpec(memory_space=pltpu.VMEM)
    args = [pltpu.with_memory_space_constraint(a, pltpu.HBM)
            for a in (rhs, factor, pivot_map, pivot_diag, pivot_off, perm)]
    hbm = pl.BlockSpec(memory_space=pltpu.HBM)
    return pl.pallas_call(
        kernel,
        out_shape=jax.ShapeDtypeStruct((BLOCKS, 1, NB, NB), F32),
        in_specs=[hbm] * 6,
        out_specs=vmem,
        scratch_shapes=[
            pltpu.VMEM((BLOCKS, NB, PANELS * NB), BF16),
            pltpu.VMEM((BLOCKS, NB, NB), BF16),
            pltpu.VMEM((PANELS, 2, NB, HALF), BF16),
            pltpu.VMEM((NB, NB), BF16), pltpu.VMEM((NB, NB), BF16),
            pltpu.VMEM((NB, NB), F32),
            pltpu.VMEM((NB, NB), BF16), pltpu.VMEM((NB, NB), BF16),
            pltpu.VMEM((NB, NB), BF16), pltpu.VMEM((NB, NB), BF16),
            pltpu.VMEM((NB, 128), F32),
            pltpu.VMEM((8, 256), F32), pltpu.VMEM((FIELDS, 8, 256), F32),
            pltpu.VMEM((PANELS * NB,), jnp.int32), pltpu.VMEM((DPART,), F32), pltpu.VMEM((DPART,), F32),
            pltpu.VMEM((PANELS, NB), jnp.int32),
            pltpu.SemaphoreType.DMA((2, BLOCKS)),
            pltpu.SemaphoreType.DMA((4,)),
            pltpu.SemaphoreType.DMA((PANELS, CHUNKS, 4)),
            pltpu.SemaphoreType.DMA((PANELS, CHUNKS)),
            pltpu.SemaphoreType.DMA((PANELS, CHUNKS)),
            pltpu.SemaphoreType.DMA((FIELDS,)), pltpu.SemaphoreType.DMA((FIELDS,)),
        ],
        compiler_params=pltpu.CompilerParams(
            collective_id=0, has_side_effects=True, vmem_limit_bytes=38 << 20),
        cost_estimate=pl.CostEstimate(flops=2 * 4096 * 1536 * 512, bytes_accessed=24 << 20, transcendentals=0),
    )(*args)


def solution(mesh):
    placed = (
        P(None, "row", None, "field"),
        P(None, "row", None, None),
        P(),
        P("field"),
        P("field"),
        P(),
    )
    return jax.shard_map(
        local, mesh=mesh, in_specs=placed, out_specs=P(None, "row", None, "field"), check_vma=False
    )
```

```python
import jax
import jax.numpy as jnp
from jax import lax
from jax.experimental import pallas as pl
from jax.experimental.pallas import tpu as pltpu
from jax.sharding import PartitionSpec as P

MESH = pl.DeviceIdType.MESH
F32, BF16 = jnp.float32, jnp.bfloat16
NB, PANELS, BLOCKS = 512, 3, 8
HALF = 256
CHUNK = 128
CHUNKS = 4
FIELDS, ROWS = 8, 16
DPART = 192

SENDS = {
    (0, 0): {0: (1,), 1: (3, 2, 5), 3: (7,), 5: (6, 4)},
    (0, 1): {0: (3,), 1: (2,), 3: (1, 4, 7), 4: (6,), 7: (5,)},
    (0, 2): {0: (3,), 3: (1, 2, 7), 7: (4, 6, 5)},
    (0, 3): {0: (4,), 3: (2, 6), 4: (3, 1, 5, 7)},
    (1, 0): {0: (4, 1), 1: (2, 5), 2: (3, 6), 4: (7,)},
    (1, 1): {0: (6, 3, 1), 1: (2,), 3: (4, 7), 4: (5,)},
    (1, 2): {0: (3, 1), 3: (4, 5, 2, 7), 7: (6,)},
    (1, 3): {0: (4, 1), 4: (7, 2, 3, 5), 7: (6,)},
    (2, 0): {0: (3, 4), 1: (0, 2, 5), 5: (6, 7)},
    (2, 1): {0: (3, 4), 1: (0, 5, 2), 5: (6, 7)},
    (2, 2): {0: (3, 4), 1: (0, 5, 2), 5: (6, 7)},
    (2, 3): {0: (3, 4), 1: (0, 5, 2), 5: (6, 7)},
}
TAKES = {
    1: ((0, 0), (1, 0), (1, 1), (0, 1), (1, 2), (0, 3), (0, 2), (1, 3)),
    2: ((0, 0), (1, 0), (0, 2), (1, 1), (1, 3), (0, 1), (1, 2), (0, 3)),
    3: ((0, 1), (0, 2), (1, 1), (1, 2), (0, 3), (0, 0), (1, 0), (1, 3)),
    4: ((0, 3), (1, 0), (1, 3), (0, 1), (1, 1), (0, 0), (1, 2), (0, 2)),
    5: ((0, 0), (1, 0), (0, 3), (1, 3), (0, 1), (1, 2), (0, 2), (1, 1)),
    6: ((1, 1), (0, 0), (1, 0), (0, 2), (0, 1), (1, 2), (0, 3), (1, 3)),
    7: ((0, 1), (0, 2), (0, 3), (1, 1), (1, 0), (1, 2), (1, 3), (0, 0)),
}
HUB_STAGE = 0
FIRST_SENT = (0, 1, 3, 2)


def dot(a, b):
    return jnp.dot(a, b, preferred_element_type=F32)


def split(a):
    high = a.astype(BF16)
    return high, (a - high.astype(F32)).astype(BF16)


def dot2(a, b):
    return dot(a[0], b) + dot(a[1], b)


def dot2r(a, b):
    return dot(a, b[0]) + dot(a, b[1])


def dot3(a, b):
    return dot(a[0], b[0]) + (dot(a[0], b[1]) + dot(a[1], b[0]))


def invert_tiles(tiles):
    rows = lax.broadcasted_iota(jnp.int32, (256, 256), 0)
    cols = lax.broadcasted_iota(jnp.int32, (256, 256), 1)
    eye = jnp.where(rows == cols, 1.0, 0.0)
    base = (rows > cols) & (rows // 16 == cols // 16)
    n1 = [jnp.where(base, t, 0.0) for t in tiles]
    n1b = [n.astype(BF16) for n in n1]
    n2 = [dot(n, n) for n in n1b]
    n2s = [split(n) for n in n2]
    n4 = [dot3(s, s) for s in n2s]
    x = [eye - a + b - dot2r(ab, bs) for a, b, ab, bs in zip(n1, n2, n1b, n2s)]
    n4s = [split(n) for n in n4]
    n8s = [split(dot3(s, s)) for s in n4s]
    x = [a + dot3(split(a), s) for a, s in zip(x, n4s)]
    x = [a + dot3(split(a), s) for a, s in zip(x, n8s)]
    size = 16
    while size < 256:
        off = (rows // (2 * size) == cols // (2 * size)) & (rows // size > cols // size)
        es = [jnp.where(off, t, 0.0).astype(BF16) for t in tiles]
        xs = [split(a) for a in x]
        ys = [split(dot2r(e, s)) for e, s in zip(es, xs)]
        x = [a - dot3(s, y) for a, s, y in zip(x, xs, ys)]
        size *= 2
    return x


def kernel(rhs, factor, pmap_hbm, pdiag_hbm, poff_hbm, perm_hbm, out, fac, b, w, xh, xl, c,
           m0h, m0l, m1h, m1l, coef, dsend, dall, pmap, pdiag, poff, perm,
           load_sem, small_sem, send_sem, recv_sem, dsend_sem, drecv_sem):
    r = lax.axis_index("row")
    f = lax.axis_index("field")
    even = lax.rem(r, 2) == 0
    odd = jnp.logical_not(even)
    solver = r < PANELS
    mate = r + 1 - 2 * lax.rem(r, 2)

    rest = pl.ds(1, BLOCKS - 1)
    loads = [pltpu.make_async_copy(src, dst, load_sem.at[k]) for k, (src, dst) in enumerate(
        ((factor.at[0, 0], fac.at[0]), (rhs.at[0, 0], b.at[0]),
         (factor.at[rest, 0], fac.at[rest]), (rhs.at[rest, 0], b.at[rest])))]
    small = [pltpu.make_async_copy(src, dst, small_sem.at[k]) for k, (src, dst) in enumerate(
        ((perm_hbm, perm), (pmap_hbm, pmap), (pdiag_hbm, pdiag), (poff_hbm, poff)))]
    loads[0].start()
    for copy in small:
        copy.start()
    loads[1].start()

    barrier = pltpu.get_barrier_semaphore()
    for k in range(1, ROWS):
        pl.semaphore_signal(barrier, inc=1, device_id=(lax.rem(r + k, ROWS), f), device_id_type=MESH)

    @pl.when(solver)
    def _():
        for k in range(1, FIELDS):
            pl.semaphore_signal(barrier, inc=1, device_id=(r, lax.rem(f + k, FIELDS)), device_id_type=MESH)

    def wslot(p, j):
        return w.at[p, j // 2, :, pl.ds((j % 2) * CHUNK, CHUNK)]

    started = [[] for _ in range(ROWS)]

    def remote(p, j, k, dst):
        return pltpu.make_async_remote_copy(
            wslot(p, j), wslot(p, j), send_sem.at[k], recv_sem.at[p, j],
            device_id=(dst, f), device_id_type=MESH)

    def start(row, p, j, dst):
        remote(p, j, len(started[row]), dst).start()
        started[row].append((p, j, dst))

    def start_mate(row, p, j):
        start(row, p, j, row ^ 1)

    def pass_on(row, p, j):
        owner = row == p
        if not owner and (row // 2 == p // 2 or row % 2 != (1 if p == 2 else 0)):
            return
        for chip in SENDS[p, j].get(row // 2, ()):
            start(row, p, j, 2 * chip + (1 if p == 2 else 0))

    def arrive(p, j):
        remote(p, j, 0, mate).wait_recv()

    def take(row, p, j):
        arrive(p, j)
        pass_on(row, p, j)
        if p == 2:
            relay = row % 2 == 1 and row != 3
        else:
            relay = row % 2 == 0 and row > 0
        if relay:
            start_mate(row, p, j)

    for copy in small + loads[:2]:
        copy.wait()
    for copy in loads[2:]:
        copy.start()

    @pl.when(solver)
    def _():
        which = lax.broadcasted_iota(jnp.int32, (128, NB), 0)
        prow = jnp.where(r == 0, perm[0:1, :], jnp.where(r == 1, perm[1:2, :], perm[2:3, :]))
        pcol = jnp.where(which == 0, prow.astype(F32), 0.0).T[:, 0:1].astype(jnp.int32)
        onehot = jnp.where(lax.broadcasted_iota(jnp.int32, (NB, NB), 1) == pcol, 1.0, 0.0).astype(BF16)
        pb = dot(onehot, b[0]).astype(BF16)

        own = pl.multiple_of(r * NB, NB)
        tiles = [fac[0, t * 256:(t + 1) * 256, pl.ds(own + t * 256, 256)].astype(F32) for t in range(2)]
        x11, x22 = invert_tiles(tiles)
        l21 = fac[0, 256:512, pl.ds(own, 256)]
        x11s, x22s = split(x11), split(x22)
        x21s = split(-dot3(x22s, split(dot2r(l21, x11s))))
        zero = jnp.zeros((256, 256), BF16)
        for ref, k in ((xh, 0), (xl, 1)):
            ref[0:256, 0:256] = x11s[k]
            ref[0:256, 256:512] = zero
            ref[256:512, 0:256] = x21s[k]
            ref[256:512, 256:512] = x22s[k]

        def apply_x(right):
            top = dot(xh[0:256, 0:256], right[0:256]) + dot(xl[0:256, 0:256], right[0:256])
            low = dot(xh[256:512, :], right) + dot(xl[256:512, :], right)
            return top, low

        top, low = apply_x(pb)
        c[0:256, :] = top
        c[256:512, :] = low

        @pl.when(r >= 1)
        def _():
            for k, part in enumerate(apply_x(fac[0, :, 0:NB])):
                m0h[k * 256:(k + 1) * 256, :], m0l[k * 256:(k + 1) * 256, :] = split(part)

        @pl.when(r >= 2)
        def _():
            for k, part in enumerate(apply_x(fac[0, :, NB:2 * NB])):
                m1h[k * 256:(k + 1) * 256, :], m1l[k * 256:(k + 1) * 256, :] = split(part)

        pl.semaphore_wait(barrier, ROWS - 1 + FIELDS - 1)

    @pl.when(jnp.logical_not(solver))
    def _():
        pl.semaphore_wait(barrier, ROWS - 1)

    def cols(j):
        return slice(j * CHUNK, (j + 1) * CHUNK)

    def wcols(p, j):
        return w[p, j // 2, :, (j % 2) * CHUNK:(j % 2 + 1) * CHUNK]

    def emit(p, j, z):
        out[0, 0, :, cols(j)] = z
        w[p, j // 2, :, (j % 2) * CHUNK:(j % 2 + 1) * CHUNK] = z.astype(BF16)

    def on_blocks(step):
        pl.when(jnp.logical_not(solver))(lambda: step(0))
        for l in range(1, BLOCKS):
            step(l)

    def trailing01(h):
        sl = slice(h * HALF, (h + 1) * HALF)

        def step(l):
            out[l, 0, :, sl] = b[l, :, sl].astype(F32) - (
                dot(fac[l, :, 0:NB], w[0, h]) + dot(fac[l, :, NB:2 * NB], w[1, h]))
        on_blocks(step)

    def trailing2(h):
        sl = slice(h * HALF, (h + 1) * HALF)

        def step(l):
            out[l, 0, :, sl] = out[l, 0, :, sl] - dot(fac[l, :, 2 * NB:3 * NB], w[2, h])
        on_blocks(step)

    @pl.when(r == 0)
    def _():
        for j in FIRST_SENT:
            emit(0, j, c[:, cols(j)])
            start_mate(0, 0, j)
            pass_on(0, 0, j)

    @pl.when(r == 1)
    def _():
        for j in range(CHUNKS):
            arrive(0, j)
            wj = wcols(0, j)
            emit(1, j, c[:, cols(j)] - (dot(m0h[...], wj) + dot(m0l[...], wj)))
            pass_on(1, 1, j)
            start_mate(1, 1, j)

    @pl.when(r == 2)
    def _():
        here = set()
        sent = 0
        for p, j in TAKES[1]:
            take(2, p, j)
            here.add((p, j))
            while (0, sent) in here and (1, sent) in here:
                w0, w1 = wcols(0, sent), wcols(1, sent)
                emit(2, sent, c[:, cols(sent)] - ((dot(m0h[...], w0) + dot(m0l[...], w0))
                                                  + (dot(m1h[...], w1) + dot(m1l[...], w1))))
                pass_on(2, 2, sent)
                start_mate(2, 2, sent)
                sent += 1

    stages = [[[] for _ in range(4)] for _ in range(ROWS)]
    last = [(2, j) for j in range(CHUNKS)]
    stages[0][0] = [(1, j) for j in range(CHUNKS)]
    for chip in range(8):
        low, high = 2 * chip, 2 * chip + 1
        if chip > 0:
            halves = [[x for x in TAKES[chip] if x[1] // 2 == h] for h in range(2)]
            passes = any(chip in SENDS[x] for x in TAKES[chip])
            if chip > 1:
                if passes:
                    stages[low][0] += TAKES[chip]
                else:
                    stages[low][0] += halves[0]
                    stages[low][1] += halves[1]
            stages[high][0] += halves[0]
            stages[high][1] += halves[1]
        hub = chip != 1 and any(chip in SENDS[x] for x in last)
        if hub:
            at = 2 if chip == 0 else HUB_STAGE
            stages[high][at] = last + stages[high][at]
        else:
            stages[high][2] += last[:2]
            stages[high][3] += last[2:]
        if chip != 1:
            stages[low][2] += last[:2]
            stages[low][3] += last[2:]

    def run_stage(k):
        for row in range(ROWS):
            if stages[row][k]:
                @pl.when(r == row)
                def _():
                    for p, j in stages[row][k]:
                        take(row, p, j)

    def dcopy(k):
        return pltpu.make_async_remote_copy(
            dsend, dall.at[f], dsend_sem.at[k], drecv_sem.at[f],
            device_id=(r, lax.rem(f + k, FIELDS)), device_id_type=MESH)

    def darrival(k):
        src = lax.rem(f + k, FIELDS)
        return pltpu.make_async_remote_copy(
            dsend, dall.at[src], dsend_sem.at[k], drecv_sem.at[src],
            device_id=(r, src), device_id_type=MESH)

    @pl.when(solver)
    def _():
        dsend[...] = jnp.zeros_like(dsend)
        dsend[0:1, 0:DPART] = pdiag[...].reshape(1, DPART)
        dsend[1:2, 0:DPART] = poff[...].reshape(1, DPART)
        for k in range(1, FIELDS):
            dcopy(k).start()

    for copy in loads[2:]:
        copy.wait()

    run_stage(0)
    trailing01(0)
    run_stage(1)
    trailing01(1)

    @pl.when(solver)
    def _():
        for k in range(1, FIELDS):
            darrival(k).wait_recv()
        for k in range(1, FIELDS):
            dcopy(k).wait_send()
        wide = jnp.zeros((8, PANELS * NB), F32)
        pad = jnp.zeros((8, PANELS * NB - 256), F32)
        for k in range(FIELDS):
            part = jnp.where(f == k, dsend[...], dall[k])
            row = jnp.concatenate([part, pad], axis=1)
            wide = wide + (pltpu.roll(row, k * DPART, 1) if k else row)

        def mine(a):
            return jnp.where(r == 0, a[:, 0:NB], jnp.where(r == 1, a[:, NB:2 * NB], a[:, 2 * NB:3 * NB]))
        both = mine(wide)
        diag, off = both[0:1], both[1:2]
        code = mine(pmap[...].reshape(1, PANELS * NB))
        diag8 = jnp.broadcast_to(diag, (8, NB))
        off8 = jnp.broadcast_to(off, (8, NB))
        code8 = jnp.broadcast_to(code, (8, NB))
        after, before = pltpu.roll(diag8, NB - 1, 1), pltpu.roll(diag8, 1, 1)
        off_before = pltpu.roll(off8, 1, 1)
        opens, closes = code8 == 1, code8 == 2
        den = jnp.where(opens, diag8 * after - off8 * off8,
                        jnp.where(closes, before * diag8 - off_before * off_before, diag8))
        own_c = jnp.where(opens, after, jnp.where(closes, before, 1.0)) / den
        next_c = jnp.where(opens, -off8, 0.0) / den
        prior_c = jnp.where(closes, -off_before, 0.0) / den
        which = lax.broadcasted_iota(jnp.int32, (128, NB), 0)
        stack = jnp.where(which == 0, own_c[0:1], jnp.where(which == 1, next_c[0:1],
                          jnp.where(which == 2, prior_c[0:1], 0.0)))
        coef[...] = stack.T
        own_k, next_k, prior_k = coef[:, 0:1], coef[:, 1:2], coef[:, 2:3]
        for j in range(CHUNKS):
            z = out[0, 0, :, cols(j)]
            out[0, 0, :, cols(j)] = (own_k * z + next_k * pltpu.roll(z, NB - 1, 0)
                                     + prior_k * pltpu.roll(z, 1, 0))

    run_stage(2)
    trailing2(0)
    run_stage(3)
    trailing2(1)

    for row in range(ROWS):
        @pl.when(r == row)
        def _():
            for k, (p, j, dst) in enumerate(started[row]):
                remote(p, j, k, dst).wait_send()


MAX_SENDS = 31


def local(rhs, factor, pivot_map, pivot_diag, pivot_off, perm):
    vmem = pl.BlockSpec(memory_space=pltpu.VMEM)
    args = [pltpu.with_memory_space_constraint(a, pltpu.HBM)
            for a in (rhs, factor, pivot_map, pivot_diag, pivot_off, perm)]
    hbm = pl.BlockSpec(memory_space=pltpu.HBM)
    return pl.pallas_call(
        kernel,
        out_shape=jax.ShapeDtypeStruct((BLOCKS, 1, NB, NB), F32),
        in_specs=[hbm] * 6,
        out_specs=vmem,
        scratch_shapes=[
            pltpu.VMEM((BLOCKS, NB, PANELS * NB), BF16),
            pltpu.VMEM((BLOCKS, NB, NB), BF16),
            pltpu.VMEM((PANELS, 2, NB, HALF), BF16),
            pltpu.VMEM((NB, NB), BF16), pltpu.VMEM((NB, NB), BF16),
            pltpu.VMEM((NB, NB), F32),
            pltpu.VMEM((NB, NB), BF16), pltpu.VMEM((NB, NB), BF16),
            pltpu.VMEM((NB, NB), BF16), pltpu.VMEM((NB, NB), BF16),
            pltpu.VMEM((NB, 128), F32),
            pltpu.VMEM((8, 256), F32), pltpu.VMEM((FIELDS, 8, 256), F32),
            pltpu.VMEM((PANELS * NB,), jnp.int32), pltpu.VMEM((DPART,), F32), pltpu.VMEM((DPART,), F32),
            pltpu.VMEM((PANELS, NB), jnp.int32),
            pltpu.SemaphoreType.DMA((4,)),
            pltpu.SemaphoreType.DMA((4,)),
            pltpu.SemaphoreType.DMA((MAX_SENDS,)),
            pltpu.SemaphoreType.DMA((PANELS, CHUNKS)),
            pltpu.SemaphoreType.DMA((FIELDS,)), pltpu.SemaphoreType.DMA((FIELDS,)),
        ],
        compiler_params=pltpu.CompilerParams(
            collective_id=0, has_side_effects=True, vmem_limit_bytes=38 << 20),
        cost_estimate=pl.CostEstimate(flops=2 * 4096 * 1536 * 512, bytes_accessed=24 << 20, transcendentals=0),
    )(*args)


def solution(mesh):
    placed = (
        P(None, "row", None, "field"),
        P(None, "row", None, None),
        P(),
        P("field"),
        P("field"),
        P(),
    )
    return jax.shard_map(
        local, mesh=mesh, in_specs=placed, out_specs=P(None, "row", None, "field"), check_vma=False
    )
```

```python
import jax
import jax.numpy as jnp
from jax import lax
from jax.experimental import pallas as pl
from jax.experimental.pallas import tpu as pltpu
from jax.sharding import PartitionSpec as P

MESH = pl.DeviceIdType.MESH
F32, BF16 = jnp.float32, jnp.bfloat16
NB, PANELS, BLOCKS = 512, 3, 8
HALF = 256
CHUNK = 128
CHUNKS = 4
FIELDS, ROWS = 8, 16
DPART = 192

SENDS = {
    (0, 0): {0: (3,), 3: (1, 7, 4, 6, 2), 7: (5,)},
    (0, 1): {0: (1,), 1: (5, 7, 2, 4), 2: (3,), 5: (6,)},
    (0, 2): {0: (4,), 3: (2,), 4: (1, 3, 5), 5: (7, 6)},
    (0, 3): {0: (4, 1), 1: (5, 2), 2: (3,), 4: (6, 7)},
    (1, 0): {0: (1, 7), 1: (2,), 7: (6, 3, 5, 4)},
    (1, 1): {0: (2, 7, 1), 2: (3, 6), 7: (5, 4)},
    (1, 2): {0: (1, 4), 4: (7, 2, 5), 7: (6, 3)},
    (1, 3): {0: (3, 1, 4), 3: (2,), 4: (7, 5), 7: (6,)},
    (2, 0): {0: (3, 4), 1: (0, 2, 5), 5: (6, 7)},
    (2, 1): {0: (3, 4), 1: (2, 5, 0), 5: (7, 6)},
    (2, 2): {0: (4, 3), 1: (0, 2, 5), 5: (6, 7)},
    (2, 3): {0: (4, 3), 1: (5, 2, 0), 5: (7, 6)},
}
TAKES = {
    1: ((0, 1), (0, 3), (1, 0), (0, 0), (1, 1), (0, 2), (1, 2), (1, 3)),
    2: ((1, 1), (0, 1), (0, 0), (0, 3), (1, 0), (1, 3), (0, 2), (1, 2)),
    3: ((0, 0), (1, 3), (0, 2), (1, 0), (1, 1), (0, 1), (0, 3), (1, 2)),
    4: ((0, 2), (0, 3), (1, 2), (1, 3), (1, 0), (0, 0), (1, 1), (0, 1)),
    5: ((0, 1), (0, 3), (0, 2), (1, 0), (1, 1), (1, 2), (0, 0), (1, 3)),
    6: ((0, 0), (1, 0), (0, 3), (1, 1), (0, 1), (0, 2), (1, 2), (1, 3)),
    7: ((1, 0), (1, 1), (0, 0), (0, 3), (0, 1), (1, 2), (1, 3), (0, 2)),
}
HUB_STAGE = 0
FIRST_SENT = (0, 1, 2, 3)


def dot(a, b):
    return jnp.dot(a, b, preferred_element_type=F32)


def split(a):
    high = a.astype(BF16)
    return high, (a - high.astype(F32)).astype(BF16)


def dot2(a, b):
    return dot(a[0], b) + dot(a[1], b)


def dot2r(a, b):
    return dot(a, b[0]) + dot(a, b[1])


def dot3(a, b):
    return dot(a[0], b[0]) + (dot(a[0], b[1]) + dot(a[1], b[0]))


def invert_tiles(tiles):
    rows = lax.broadcasted_iota(jnp.int32, (256, 256), 0)
    cols = lax.broadcasted_iota(jnp.int32, (256, 256), 1)
    eye = jnp.where(rows == cols, 1.0, 0.0)
    base = (rows > cols) & (rows // 16 == cols // 16)
    n1 = [jnp.where(base, t, 0.0) for t in tiles]
    n1b = [n.astype(BF16) for n in n1]
    n2 = [dot(n, n) for n in n1b]
    n2s = [split(n) for n in n2]
    n4 = [dot3(s, s) for s in n2s]
    x = [eye - a + b - dot2r(ab, bs) for a, b, ab, bs in zip(n1, n2, n1b, n2s)]
    n4s = [split(n) for n in n4]
    n8s = [split(dot3(s, s)) for s in n4s]
    x = [a + dot3(split(a), s) for a, s in zip(x, n4s)]
    x = [a + dot3(split(a), s) for a, s in zip(x, n8s)]
    size = 16
    while size < 256:
        off = (rows // (2 * size) == cols // (2 * size)) & (rows // size > cols // size)
        es = [jnp.where(off, t, 0.0).astype(BF16) for t in tiles]
        xs = [split(a) for a in x]
        ys = [split(dot2r(e, s)) for e, s in zip(es, xs)]
        x = [a - dot3(s, y) for a, s, y in zip(x, xs, ys)]
        size *= 2
    return x


def kernel(rhs, factor, pmap_hbm, pdiag_hbm, poff_hbm, perm_hbm, out, fac, b, w, xh, xl, c,
           m0h, m0l, m1h, m1l, coef, dsend, dall, pmap, pdiag, poff, perm,
           load_sem, small_sem, send_sem, recv_sem, dsend_sem, drecv_sem):
    r = lax.axis_index("row")
    f = lax.axis_index("field")
    even = lax.rem(r, 2) == 0
    odd = jnp.logical_not(even)
    solver = r < PANELS
    mate = r + 1 - 2 * lax.rem(r, 2)

    rest = pl.ds(1, BLOCKS - 1)
    loads = [pltpu.make_async_copy(src, dst, load_sem.at[k]) for k, (src, dst) in enumerate(
        ((factor.at[0, 0], fac.at[0]), (rhs.at[0, 0], b.at[0]),
         (factor.at[rest, 0], fac.at[rest]), (rhs.at[rest, 0], b.at[rest])))]
    small = [pltpu.make_async_copy(src, dst, small_sem.at[k]) for k, (src, dst) in enumerate(
        ((perm_hbm, perm), (pmap_hbm, pmap), (pdiag_hbm, pdiag), (poff_hbm, poff)))]
    loads[0].start()
    for copy in small:
        copy.start()
    loads[1].start()

    barrier = pltpu.get_barrier_semaphore()
    for k in range(1, ROWS):
        pl.semaphore_signal(barrier, inc=1, device_id=(lax.rem(r + k, ROWS), f), device_id_type=MESH)

    @pl.when(solver)
    def _():
        for k in range(1, FIELDS):
            pl.semaphore_signal(barrier, inc=1, device_id=(r, lax.rem(f + k, FIELDS)), device_id_type=MESH)

    def wslot(p, j):
        return w.at[p, j // 2, :, pl.ds((j % 2) * CHUNK, CHUNK)]

    started = [[] for _ in range(ROWS)]

    def remote(p, j, k, dst):
        return pltpu.make_async_remote_copy(
            wslot(p, j), wslot(p, j), send_sem.at[k], recv_sem.at[p, j],
            device_id=(dst, f), device_id_type=MESH)

    def start(row, p, j, dst):
        remote(p, j, len(started[row]), dst).start()
        started[row].append((p, j, dst))

    def start_mate(row, p, j):
        start(row, p, j, row ^ 1)

    def pass_on(row, p, j):
        owner = row == p
        if not owner and (row // 2 == p // 2 or row % 2 != (1 if p == 2 else 0)):
            return
        for chip in SENDS[p, j].get(row // 2, ()):
            start(row, p, j, 2 * chip + (1 if p == 2 else 0))

    def arrive(p, j):
        remote(p, j, 0, mate).wait_recv()

    def take(row, p, j):
        arrive(p, j)
        pass_on(row, p, j)
        if p == 2:
            relay = row % 2 == 1 and row != 3
        else:
            relay = row % 2 == 0 and row > 0
        if relay:
            start_mate(row, p, j)

    for copy in small + loads[:2]:
        copy.wait()
    for copy in loads[2:]:
        copy.start()

    @pl.when(solver)
    def _():
        which = lax.broadcasted_iota(jnp.int32, (128, NB), 0)
        prow = jnp.where(r == 0, perm[0:1, :], jnp.where(r == 1, perm[1:2, :], perm[2:3, :]))
        pcol = jnp.where(which == 0, prow.astype(F32), 0.0).T[:, 0:1].astype(jnp.int32)
        onehot = jnp.where(lax.broadcasted_iota(jnp.int32, (NB, NB), 1) == pcol, 1.0, 0.0).astype(BF16)
        pb = dot(onehot, b[0]).astype(BF16)

        own = pl.multiple_of(r * NB, NB)
        tiles = [fac[0, t * 256:(t + 1) * 256, pl.ds(own + t * 256, 256)].astype(F32) for t in range(2)]
        x11, x22 = invert_tiles(tiles)
        l21 = fac[0, 256:512, pl.ds(own, 256)]
        x11s, x22s = split(x11), split(x22)
        x21s = split(-dot3(x22s, split(dot2r(l21, x11s))))
        zero = jnp.zeros((256, 256), BF16)
        for ref, k in ((xh, 0), (xl, 1)):
            ref[0:256, 0:256] = x11s[k]
            ref[0:256, 256:512] = zero
            ref[256:512, 0:256] = x21s[k]
            ref[256:512, 256:512] = x22s[k]

        def apply_x(right):
            top = dot(xh[0:256, 0:256], right[0:256]) + dot(xl[0:256, 0:256], right[0:256])
            low = dot(xh[256:512, :], right) + dot(xl[256:512, :], right)
            return top, low

        top, low = apply_x(pb)
        c[0:256, :] = top
        c[256:512, :] = low

        @pl.when(r >= 1)
        def _():
            for k, part in enumerate(apply_x(fac[0, :, 0:NB])):
                m0h[k * 256:(k + 1) * 256, :], m0l[k * 256:(k + 1) * 256, :] = split(part)

        @pl.when(r >= 2)
        def _():
            for k, part in enumerate(apply_x(fac[0, :, NB:2 * NB])):
                m1h[k * 256:(k + 1) * 256, :], m1l[k * 256:(k + 1) * 256, :] = split(part)

        pl.semaphore_wait(barrier, ROWS - 1 + FIELDS - 1)

    @pl.when(jnp.logical_not(solver))
    def _():
        pl.semaphore_wait(barrier, ROWS - 1)

    def cols(j):
        return slice(j * CHUNK, (j + 1) * CHUNK)

    def wcols(p, j):
        return w[p, j // 2, :, (j % 2) * CHUNK:(j % 2 + 1) * CHUNK]

    def emit(p, j, z):
        out[0, 0, :, cols(j)] = z
        w[p, j // 2, :, (j % 2) * CHUNK:(j % 2 + 1) * CHUNK] = z.astype(BF16)

    def on_blocks(step):
        pl.when(jnp.logical_not(solver))(lambda: step(0))
        for l in range(1, BLOCKS):
            step(l)

    def trailing01(h):
        sl = slice(h * HALF, (h + 1) * HALF)

        def step(l):
            out[l, 0, :, sl] = b[l, :, sl].astype(F32) - (
                dot(fac[l, :, 0:NB], w[0, h]) + dot(fac[l, :, NB:2 * NB], w[1, h]))
        on_blocks(step)

    def trailing2(h):
        sl = slice(h * HALF, (h + 1) * HALF)

        def step(l):
            out[l, 0, :, sl] = out[l, 0, :, sl] - dot(fac[l, :, 2 * NB:3 * NB], w[2, h])
        on_blocks(step)

    @pl.when(r == 0)
    def _():
        for j in FIRST_SENT:
            emit(0, j, c[:, cols(j)])
            start_mate(0, 0, j)
            pass_on(0, 0, j)

    @pl.when(r == 1)
    def _():
        for j in range(CHUNKS):
            arrive(0, j)
            wj = wcols(0, j)
            emit(1, j, c[:, cols(j)] - (dot(m0h[...], wj) + dot(m0l[...], wj)))
            pass_on(1, 1, j)
            start_mate(1, 1, j)

    @pl.when(r == 2)
    def _():
        here = set()
        sent = 0
        for p, j in TAKES[1]:
            take(2, p, j)
            here.add((p, j))
            while (0, sent) in here and (1, sent) in here:
                w0, w1 = wcols(0, sent), wcols(1, sent)
                emit(2, sent, c[:, cols(sent)] - ((dot(m0h[...], w0) + dot(m0l[...], w0))
                                                  + (dot(m1h[...], w1) + dot(m1l[...], w1))))
                pass_on(2, 2, sent)
                start_mate(2, 2, sent)
                sent += 1

    stages = [[[] for _ in range(4)] for _ in range(ROWS)]
    last = [(2, j) for j in range(CHUNKS)]
    stages[0][0] = [(1, j) for j in range(CHUNKS)]
    for chip in range(8):
        low, high = 2 * chip, 2 * chip + 1
        if chip > 0:
            halves = [[x for x in TAKES[chip] if x[1] // 2 == h] for h in range(2)]
            passes = any(chip in SENDS[x] for x in TAKES[chip])
            if chip > 1:
                if passes:
                    stages[low][0] += TAKES[chip]
                else:
                    stages[low][0] += halves[0]
                    stages[low][1] += halves[1]
            stages[high][0] += halves[0]
            stages[high][1] += halves[1]
        hub = chip != 1 and any(chip in SENDS[x] for x in last)
        if hub:
            at = 2 if chip == 0 else HUB_STAGE
            stages[high][at] = last + stages[high][at]
        else:
            stages[high][2] += last[:2]
            stages[high][3] += last[2:]
        if chip != 1:
            stages[low][2] += last[:2]
            stages[low][3] += last[2:]

    def run_stage(k):
        for row in range(ROWS):
            if stages[row][k]:
                @pl.when(r == row)
                def _():
                    for p, j in stages[row][k]:
                        take(row, p, j)

    def dcopy(k):
        return pltpu.make_async_remote_copy(
            dsend, dall.at[f], dsend_sem.at[k], drecv_sem.at[f],
            device_id=(r, lax.rem(f + k, FIELDS)), device_id_type=MESH)

    def darrival(k):
        src = lax.rem(f + k, FIELDS)
        return pltpu.make_async_remote_copy(
            dsend, dall.at[src], dsend_sem.at[k], drecv_sem.at[src],
            device_id=(r, src), device_id_type=MESH)

    @pl.when(solver)
    def _():
        dsend[...] = jnp.zeros_like(dsend)
        dsend[0:1, 0:DPART] = pdiag[...].reshape(1, DPART)
        dsend[1:2, 0:DPART] = poff[...].reshape(1, DPART)
        for k in range(1, FIELDS):
            dcopy(k).start()

    for copy in loads[2:]:
        copy.wait()

    run_stage(0)
    trailing01(0)
    run_stage(1)
    trailing01(1)

    @pl.when(solver)
    def _():
        for k in range(1, FIELDS):
            darrival(k).wait_recv()
        for k in range(1, FIELDS):
            dcopy(k).wait_send()
        wide = jnp.zeros((8, PANELS * NB), F32)
        pad = jnp.zeros((8, PANELS * NB - 256), F32)
        for k in range(FIELDS):
            part = jnp.where(f == k, dsend[...], dall[k])
            row = jnp.concatenate([part, pad], axis=1)
            wide = wide + (pltpu.roll(row, k * DPART, 1) if k else row)

        def mine(a):
            return jnp.where(r == 0, a[:, 0:NB], jnp.where(r == 1, a[:, NB:2 * NB], a[:, 2 * NB:3 * NB]))
        both = mine(wide)
        diag, off = both[0:1], both[1:2]
        code = mine(pmap[...].reshape(1, PANELS * NB))
        diag8 = jnp.broadcast_to(diag, (8, NB))
        off8 = jnp.broadcast_to(off, (8, NB))
        code8 = jnp.broadcast_to(code, (8, NB))
        after, before = pltpu.roll(diag8, NB - 1, 1), pltpu.roll(diag8, 1, 1)
        off_before = pltpu.roll(off8, 1, 1)
        opens, closes = code8 == 1, code8 == 2
        den = jnp.where(opens, diag8 * after - off8 * off8,
                        jnp.where(closes, before * diag8 - off_before * off_before, diag8))
        own_c = jnp.where(opens, after, jnp.where(closes, before, 1.0)) / den
        next_c = jnp.where(opens, -off8, 0.0) / den
        prior_c = jnp.where(closes, -off_before, 0.0) / den
        which = lax.broadcasted_iota(jnp.int32, (128, NB), 0)
        stack = jnp.where(which == 0, own_c[0:1], jnp.where(which == 1, next_c[0:1],
                          jnp.where(which == 2, prior_c[0:1], 0.0)))
        coef[...] = stack.T
        own_k, next_k, prior_k = coef[:, 0:1], coef[:, 1:2], coef[:, 2:3]
        for j in range(CHUNKS):
            z = out[0, 0, :, cols(j)]
            out[0, 0, :, cols(j)] = (own_k * z + next_k * pltpu.roll(z, NB - 1, 0)
                                     + prior_k * pltpu.roll(z, 1, 0))

    run_stage(2)
    trailing2(0)
    run_stage(3)
    trailing2(1)

    for row in range(ROWS):
        @pl.when(r == row)
        def _():
            for k, (p, j, dst) in enumerate(started[row]):
                remote(p, j, k, dst).wait_send()


MAX_SENDS = 31


def local(rhs, factor, pivot_map, pivot_diag, pivot_off, perm):
    vmem = pl.BlockSpec(memory_space=pltpu.VMEM)
    args = [pltpu.with_memory_space_constraint(a, pltpu.HBM)
            for a in (rhs, factor, pivot_map, pivot_diag, pivot_off, perm)]
    hbm = pl.BlockSpec(memory_space=pltpu.HBM)
    return pl.pallas_call(
        kernel,
        out_shape=jax.ShapeDtypeStruct((BLOCKS, 1, NB, NB), F32),
        in_specs=[hbm] * 6,
        out_specs=vmem,
        scratch_shapes=[
            pltpu.VMEM((BLOCKS, NB, PANELS * NB), BF16),
            pltpu.VMEM((BLOCKS, NB, NB), BF16),
            pltpu.VMEM((PANELS, 2, NB, HALF), BF16),
            pltpu.VMEM((NB, NB), BF16), pltpu.VMEM((NB, NB), BF16),
            pltpu.VMEM((NB, NB), F32),
            pltpu.VMEM((NB, NB), BF16), pltpu.VMEM((NB, NB), BF16),
            pltpu.VMEM((NB, NB), BF16), pltpu.VMEM((NB, NB), BF16),
            pltpu.VMEM((NB, 128), F32),
            pltpu.VMEM((8, 256), F32), pltpu.VMEM((FIELDS, 8, 256), F32),
            pltpu.VMEM((PANELS * NB,), jnp.int32), pltpu.VMEM((DPART,), F32), pltpu.VMEM((DPART,), F32),
            pltpu.VMEM((PANELS, NB), jnp.int32),
            pltpu.SemaphoreType.DMA((4,)),
            pltpu.SemaphoreType.DMA((4,)),
            pltpu.SemaphoreType.DMA((MAX_SENDS,)),
            pltpu.SemaphoreType.DMA((PANELS, CHUNKS)),
            pltpu.SemaphoreType.DMA((FIELDS,)), pltpu.SemaphoreType.DMA((FIELDS,)),
        ],
        compiler_params=pltpu.CompilerParams(
            collective_id=0, has_side_effects=True, vmem_limit_bytes=38 << 20),
        cost_estimate=pl.CostEstimate(flops=2 * 4096 * 1536 * 512, bytes_accessed=24 << 20, transcendentals=0),
    )(*args)


def solution(mesh):
    placed = (
        P(None, "row", None, "field"),
        P(None, "row", None, None),
        P(),
        P("field"),
        P("field"),
        P(),
    )
    return jax.shard_map(
        local, mesh=mesh, in_specs=placed, out_specs=P(None, "row", None, "field"), check_vma=False
    )
```
